512 devices in a mesh: row: 2 (over z_hi), head: 8 (over y, core), seq: 32 (over x, z_lo).
Axes of the slice: x: 4, y: 4, z: 16 (z_hi: 2, z_lo: 8; z = z_hi * 8 + z_lo), core: 2. Of those that a mesh axis runs over, the one named last changes fastest.
Arguments:
- queries: bfloat16 [64, 256, 3072], P(('row', 'seq'), 'head'), parts along dimension 0, may hold values from -45 to 45
- keys: bfloat16 [64, 256, 3072], P(('row', 'seq'), 'head'), parts along dimension 0, may hold values from -6 to 6
- values: bfloat16 [64, 256, 3072], P(('row', 'seq'), 'head'), parts along dimension 0, may hold values from -6 to 6
- clip_lengths: int32 [12], P('row'), parts along dimension 0, may hold values from 1 to 5120, 8192 in all
Outputs:
- attended: bfloat16 [64, 256, 3072], P(('row', 'seq'), 'head'), parts along dimension 0
The draws below stay inside these ranges and needn't reach their ends.
There are 2 independent parts, one for each index of `row`. The reference program is written for one: setup_inputs(seed, part) draws one part's arguments, and reference() takes and returns one part's arrays. A program takes and returns all parts, laid end to end along the dimension named above; each array names one. Nothing has to cross between parts.
All inputs are finite; a program needn't handle non-finite values.
Results may differ from the reference program's by a relative error of at most 0.0065.
Values may be sent and summed in bfloat16 or wider, within the bound.
A program may use at most 128 MiB of HBM per device.

```python
import math
import jax
import jax.numpy as jnp
import numpy as np
from jax import lax

HEAD = 128
HEADS = 24
CLIPS = 6
TOK_DEV = 256
WIDTH = 3072
BLOCKS = 32
TOKENS = 8192
MOST = 5120


def draw_keys(key, part):
    key = jax.random.fold_in(key, 5)
    out = jnp.clip(jax.random.normal(key, (TOKENS, WIDTH), jnp.float32), -6.0, 6.0)
    return out.reshape(BLOCKS, TOK_DEV, WIDTH).astype(jnp.bfloat16)


def draw_queries(key, part):
    key = jax.random.fold_in(key, 7)
    out = jnp.clip(jax.random.normal(key, (TOKENS, WIDTH), jnp.float32), -6.0, 6.0)
    return out.reshape(BLOCKS, TOK_DEV, WIDTH).astype(jnp.bfloat16)


def block_levels(key, shape, cuts, least, top_value):
    def one(axis_at, parts):
        steps = jax.random.uniform(jax.random.fold_in(jax.random.fold_in(key, 6), axis_at), (parts,), jnp.float32, least / len(cuts), top_value / len(cuts))
        return jnp.repeat(jnp.exp(steps), shape[axis_at] // parts).reshape((-1,) + (1,) * (len(shape) - axis_at - 1))

    factor_of = one(*cuts[0])
    for cut in cuts[1:]:
        factor_of = factor_of * one(*cut)
    return factor_of


def split_up(amount, total, most, lean):
    portions = [(1 << 20) // math.isqrt(standing ** lean) + 1 for standing in range(2, amount + 1)]
    spare, counts = total - most - (amount - 1), [1] * (amount - 1)
    while spare > 0:
        free = [i for i in range(amount - 1) if counts[i] < most]
        mass, budget = sum([portions[i] for i in free]), spare
        for i in free:
            more = min(most - counts[i], max(1, budget * portions[i] // mass), spare)
            counts[i] = counts[i] + more
            spare = spare - more
    return np.array([most] + counts)


def uneven(own_key, count, total, limit, skew):
    if count == 2:
        one = jax.random.randint(own_key, (), max(1, total - limit), min(limit, total - 1) + 1)
        return jnp.stack([one, total - one])
    tallies = jnp.asarray(split_up(count, total, limit, skew), jnp.int32)
    twos = (count - 1) // 2
    source_of, taker = tallies[1:1 + 2 * twos:2], tallies[2:2 + 2 * twos:2]
    slack = jnp.minimum(source_of - 1, limit - taker)
    shifted = jax.random.randint(jax.random.fold_in(own_key, 1), (twos,), 0, 1 << 20) % (slack + 1)
    tallies = tallies.at[1:1 + 2 * twos:2].set(source_of - shifted).at[2:2 + 2 * twos:2].set(taker + shifted)
    return tallies[jax.random.permutation(jax.random.fold_in(own_key, 2), count)]


def normal_values(rng, extent, scale, limit, pieces=(), kind=jnp.bfloat16):
    level = block_levels(rng, extent, pieces, -0.22, 0.18) if pieces else 1.0
    array = jax.random.normal(rng, extent, jnp.float32) * scale * level
    return jnp.minimum(jnp.maximum(array, -limit), limit).astype(kind)


def setup_inputs(seed: int = 0, part: int = 0) -> dict:
    key_list = jax.random.split(jax.random.key(seed), 5)
    own_keys = jax.random.split(jax.random.fold_in(key_list[4], part), 5)
    return {
        "queries": draw_queries(jax.random.fold_in(jax.random.fold_in(key_list[4], part), 71), part),
        "keys": draw_keys(jax.random.fold_in(jax.random.fold_in(key_list[4], part), 71), part),
        "values": normal_values(own_keys[2], (BLOCKS, TOK_DEV, WIDTH), 1.0, 6.0, ((0, 32), (1, 8))),
        "clip_lengths": uneven(own_keys[3], CLIPS, TOKENS, MOST, 2).astype(jnp.int32),
    }


def clip_index(clip_lengths):
    ends = jnp.cumsum(clip_lengths)
    pos = jnp.arange(TOKENS, dtype=jnp.int32)
    return jnp.sum((pos[:, None] >= ends[None, :]).astype(jnp.int32), axis=1)


def reference(queries, keys, values, clip_lengths):
    clips = clip_index(clip_lengths)
    same = clips[:, None] == clips[None, :]
    q_all = queries.reshape(TOKENS, HEADS, HEAD).transpose(1, 0, 2)
    k_all = keys.reshape(TOKENS, HEADS, HEAD).transpose(1, 0, 2)
    v_all = values.reshape(TOKENS, HEADS, HEAD).transpose(1, 0, 2)

    def one_head(items):
        q_head, k_head, v_head = items
        score = jnp.dot(q_head, k_head.T, preferred_element_type=jnp.float32) * (HEAD ** -0.5)
        score = jnp.where(same, score, jnp.float32(-1e30))
        top = jnp.max(score, axis=1, keepdims=True)
        weight = jnp.where(same, jnp.exp(score - top), jnp.float32(0.0))
        total = jnp.sum(weight, axis=1, keepdims=True)
        numer = jnp.dot(weight.astype(jnp.bfloat16), v_head, preferred_element_type=jnp.float32)
        return (numer / total).astype(jnp.bfloat16)

    result = lax.map(one_head, (q_all, k_all, v_all))
    return result.transpose(1, 0, 2).reshape(BLOCKS, TOK_DEV, WIDTH)
```

```python
import jax
import jax.numpy as jnp
from jax import lax
from jax.experimental import pallas as pl
from jax.experimental.pallas import tpu as pltpu
from jax.sharding import PartitionSpec as P

HEAD = 128
NX, NY, NZ, NC = 4, 4, 8, 2
PER = 3
RUN = 32
CLIPS = 6
OFFSETS = (0, 4, 3, 5, 2, 6, 1, 7)
FAR = 131072.0
SCALE = HEAD**-0.5 * 1.4426950408889634
MESH = pl.DeviceIdType.MESH
KEYS_STEP = 4
QUERY_STEP = 4


def kernel(len_ref, q_ref, k_ref, v_ref, out_ref, kv, qs, far, score, result, *sems):
    send_kv, send_q, send_x, send_c, send_o, recv_kv, recv_q, recv_x, recv_c, recv_o = sems
    seq, head = lax.axis_index("seq"), lax.axis_index("head")
    x, z = seq // NZ, seq % NZ
    y, c = head // NC, head % NC
    mine = (y + NZ - z - 1) % NY
    active = mine < PER
    right, left, across = (x + 1) % NX, (x + 3) % NX, (x + 2) % NX

    def at(x_, y_, z_, c_):
        return {"seq": x_ * NZ + z_, "head": y_ * NC + c_}

    def remote(src, dst, send, recv, device):
        return pltpu.make_async_remote_copy(
            src_ref=src, dst_ref=dst, send_sem=send, recv_sem=recv, device_id=device, device_id_type=MESH
        )

    def landed(ref, sem):
        pltpu.make_async_copy(ref, ref, sem).wait()

    barrier = pltpu.get_barrier_semaphore()
    for dz in range(NZ):
        for dy in range(NY):
            if dz or dy:
                pl.semaphore_signal(
                    barrier, inc=1, device_id=at(x, (y + dy) % NY, (z + dz) % NZ, c), device_id_type=MESH
                )
    for device in (at(right, y, z, c), at(left, y, z, c), at(x, y, z, 1 - c)):
        pl.semaphore_signal(barrier, inc=1, device_id=device, device_id_type=MESH)
    pl.semaphore_wait(barrier, NZ * NY - 1 + 3)

    def columns(z_, h):
        return pl.ds(pl.multiple_of((z_ * PER + h) * HEAD, HEAD), HEAD)

    def outgoing(i, h, queries):
        z_ = (z + OFFSETS[i]) % NZ
        device = at(x, (z_ + 1 + h) % NY, z_, c)
        cols = columns(z_, h)
        if queries:
            return [(q_ref.at[0, :, cols], qs.at[i, y], send_q.at[i, h], recv_q.at[i], device)]
        return [
            (ref.at[0, :, cols], kv.at[n, i, x, c, y], send_kv.at[i, h, n], recv_kv.at[i], device)
            for n, ref in enumerate((k_ref, v_ref))
        ]

    def send(i, queries):
        for h in range(PER):
            for src, dst, out, into, device in outgoing(i, h, queries):
                if i == 0:
                    pl.when(mine == h)(lambda: pltpu.make_async_copy(src, dst, into).start())
                    pl.when(mine != h)(lambda: remote(src, dst, out, into, device).start())
                else:
                    remote(src, dst, out, into, device).start()

    def sent(i, queries):
        for h in range(PER):
            for src, dst, out, into, device in outgoing(i, h, queries):
                if i == 0:
                    pl.when(mine != h)(lambda: remote(src, dst, out, into, device).wait_send())
                else:
                    remote(src, dst, out, into, device).wait_send()

    for i in range(NZ):
        send(i, False)

    def along_x(i):
        own, from_left, from_right = kv.at[:, i, x, c], kv.at[0, i, left, c], kv.at[1, i, right, c]
        return [
            remote(own, own, send_x.at[i, 0], recv_x.at[i, 0], at(right, y, z, c)),
            remote(own, own, send_x.at[i, 1], recv_x.at[i, 1], at(left, y, z, c)),
            remote(from_left, from_left, send_x.at[i, 2], recv_x.at[i, 2], at(right, y, z, c)),
            remote(from_right, from_right, send_x.at[i, 3], recv_x.at[i, 3], at(left, y, z, c)),
        ]

    def to_core(i, n):
        ref = kv.at[:, i, (x, left, right, across)[n], c]
        return remote(ref, ref, send_c.at[i, n], recv_c.at[i], at(x, y, z, 1 - c))

    lane = lax.broadcasted_iota(jnp.int32, (1, HEAD), 1)
    first, last = jnp.zeros((1, HEAD), jnp.int32), jnp.full((1, HEAD), 1 << 20, jnp.int32)
    end = 0
    for n in range(CLIPS):
        start, end = end, end + len_ref[n]
        first = jnp.where(lane == n, start, first)
        last = jnp.where(lane == n, end, last)

    def within(position):
        return (position >= first) & (position < last)

    def far_keys(i):
        row = lax.broadcasted_iota(jnp.int32, (NX * NC * NY * RUN, HEAD), 0)
        slab = (z + NZ - OFFSETS[i]) % NZ
        position = ((row >> 8) << 11) + (((row >> 5) & 3) << 6) + (((row >> 7) & 1) << 5) + (row & 31) + slab * 256
        far[i] = jnp.where(within(position), 0.0, -FAR).astype(jnp.bfloat16)

    def clip_queries(i):
        row = lax.broadcasted_iota(jnp.int32, (NY * RUN, HEAD), 0)
        slab = (z + NZ - OFFSETS[i]) % NZ
        position = ((row >> 5) << 6) + (row & 31) + (x * 2048 + slab * 256 + c * 32)
        return jnp.where(within(position), 1.0, 0.0).astype(jnp.bfloat16)

    @pl.when(jnp.logical_not(active))
    def _():
        for i in range(NZ):
            sent(i, False)
            send(i, True)

    @pl.when(active)
    def _():
        for i in range(NZ):
            far_keys(i)
        for t in range(NZ + 3):
            if t < NZ:
                landed(kv.at[:, t, x, c], recv_kv.at[t])
                for copy in along_x(t)[:2]:
                    copy.start()
                to_core(t, 0).start()
                sent(t, False)
                send(t, True)
            if 1 <= t < NZ + 1:
                landed(kv.at[:, t - 1, left, c], recv_x.at[t - 1, 0])
                landed(kv.at[:, t - 1, right, c], recv_x.at[t - 1, 1])
                for copy in along_x(t - 1)[2:]:
                    copy.start()
                to_core(t - 1, 1).start()
                to_core(t - 1, 2).start()
            if 2 <= t < NZ + 2:
                landed(kv.at[0, t - 2, across, c], recv_x.at[t - 2, 2])
                landed(kv.at[1, t - 2, across, c], recv_x.at[t - 2, 3])
                to_core(t - 2, 3).start()
            if t >= 3:
                landed(kv.at[:, t - 3, :, 1 - c], recv_c.at[t - 3])

    def results(i):
        z_ = (z + NZ - OFFSETS[i]) % NZ
        dst = out_ref.at[0, :, columns(z, mine)]
        return [(result.at[i, n], dst, send_o.at[i, n], recv_o, at(x, n, z_, c)) for n in range(NY)]

    @pl.when(active)
    def _():
        keys = KEYS_STEP * NX * NC * NY * RUN
        rows = QUERY_STEP * NY * RUN
        for b in range(NZ // QUERY_STEP):
            rounds = range(b * QUERY_STEP, (b + 1) * QUERY_STEP)
            for i in rounds:
                landed(qs.at[i], recv_q.at[i])
            query = jnp.concatenate(
                [
                    qs[b * QUERY_STEP : (b + 1) * QUERY_STEP].reshape(rows, HEAD),
                    jnp.concatenate([clip_queries(i) for i in rounds], axis=0),
                ],
                axis=1,
            )

            def scores(j, top):
                part = pl.ds(j * KEYS_STEP, KEYS_STEP)
                key = jnp.concatenate([kv[0, part].reshape(keys, HEAD), far[part].reshape(keys, HEAD)], axis=1)
                got = lax.dot_general(query, key, (((1,), (1,)), ((), ())), preferred_element_type=jnp.float32)
                score[j] = got
                for n in range(keys // HEAD):
                    top = jnp.maximum(top, got[:, n * HEAD : (n + 1) * HEAD])
                return top

            steps = NZ // KEYS_STEP
            top = lax.fori_loop(0, steps, scores, jnp.full((rows, HEAD), -1e30, jnp.float32))
            top = jnp.max(top, axis=1, keepdims=True)

            def attend(j, total):
                part = pl.ds(j * KEYS_STEP, KEYS_STEP)
                weight = jnp.exp2((score[j] - top) * SCALE).astype(jnp.bfloat16)
                value = jnp.concatenate(
                    [kv[1, part].reshape(keys, HEAD), jnp.ones((keys, HEAD), jnp.bfloat16)], axis=1
                )
                return total + jnp.dot(weight, value, preferred_element_type=jnp.float32)

            total = lax.fori_loop(0, steps, attend, jnp.zeros((rows, 2 * HEAD), jnp.float32))
            ready = (total[:, :HEAD] / total[:, HEAD:]).astype(jnp.bfloat16)
            result[b * QUERY_STEP : (b + 1) * QUERY_STEP] = ready.reshape(QUERY_STEP, NY, RUN, HEAD)
            for i in rounds:
                for n, (src, dst, out, into, device) in enumerate(results(i)):
                    if i == 0:
                        pl.when(y == n)(lambda: pltpu.make_async_copy(src, dst, into).start())
                        pl.when(y != n)(lambda: remote(src, dst, out, into, device).start())
                    else:
                        remote(src, dst, out, into, device).start()

    landed(out_ref, recv_o)
    for i in range(NZ):
        sent(i, True)

    @pl.when(active)
    def _():
        for i in range(NZ):
            for copy in along_x(i):
                copy.wait_send()
            for n in range(4):
                to_core(i, n).wait_send()
            for n, (src, dst, out, into, device) in enumerate(results(i)):
                if i == 0:
                    pl.when(y != n)(lambda: remote(src, dst, out, into, device).wait_send())
                else:
                    remote(src, dst, out, into, device).wait_send()


def shards(queries, keys, values, clip_lengths):
    width = queries.shape[2]
    dma = pltpu.SemaphoreType.DMA
    query_rows, key_rows = QUERY_STEP * NY * RUN, KEYS_STEP * NX * NC * NY * RUN
    vmem = pl.BlockSpec(memory_space=pltpu.VMEM)
    return pl.pallas_call(
        kernel,
        out_shape=jax.ShapeDtypeStruct((1, RUN, width), jnp.bfloat16),
        in_specs=[pl.BlockSpec(memory_space=pltpu.SMEM), vmem, vmem, vmem],
        out_specs=vmem,
        scratch_shapes=[
            pltpu.VMEM((2, NZ, NX, NC, NY, RUN, HEAD), jnp.bfloat16),
            pltpu.VMEM((NZ, NY, RUN, HEAD), jnp.bfloat16),
            pltpu.VMEM((NZ, NX * NC * NY * RUN, HEAD), jnp.bfloat16),
            pltpu.VMEM((NZ // KEYS_STEP, query_rows, key_rows), jnp.float32),
            pltpu.VMEM((NZ, NY, RUN, HEAD), jnp.bfloat16),
            dma((NZ, PER, 2)),
            dma((NZ, PER)),
            dma((NZ, 4)),
            dma((NZ, 4)),
            dma((NZ, NY)),
            dma((NZ,)),
            dma((NZ,)),
            dma((NZ, 4)),
            dma((NZ,)),
            dma,
        ],
        compiler_params=pltpu.CompilerParams(
            collective_id=0, has_side_effects=True, vmem_limit_bytes=56 * 2**20
        ),
        cost_estimate=pl.CostEstimate(flops=2 * 1024 * 8192 * 512, bytes_accessed=2**20, transcendentals=2**23),
    )(clip_lengths, queries, keys, values)


def solution(mesh):
    spec = P(("row", "seq"), "head", None)
    return jax.shard_map(
        shards, mesh=mesh, in_specs=(spec, spec, spec, P("row")), out_specs=spec, check_vma=False
    )
```

```python
import jax
import jax.numpy as jnp
from jax import lax
from jax.experimental import pallas as pl
from jax.experimental.pallas import tpu as pltpu
from jax.sharding import PartitionSpec as P

HEAD = 128
NX, NY, NZ, NC = 4, 4, 8, 2
PER = 3
RUN = 32
CLIPS = 6
OFFSETS = (0, 1, 7, 2, 6, 3, 5, 4)
FAR = 131072.0
SCALE = HEAD**-0.5 * 1.4426950408889634
MESH = pl.DeviceIdType.MESH
KEYS = NX * NC * NY * RUN
KEYS_STEP = 2
QUERY_STEP = 2
UNITS = [(n, i) for n in (0, 2, 1) for i in range(NZ)]
WINDOW = 16
LAG = 4
SCORES_AT = 12


def kernel(len_ref, q_ref, k_ref, v_ref, out_ref, kv, qs, far, query, score, top, result, landing, *sems):
    send_z, send_x, send_c, send_o, recv_z, recv_x, recv_c, recv_o = sems
    seq, head = lax.axis_index("seq"), lax.axis_index("head")
    x, z = seq // NZ, seq % NZ
    y, c = head // NC, head % NC
    mine = (y + NZ - z - 1) % NY
    active = mine < PER
    right, left, across = (x + 1) % NX, (x + 3) % NX, (x + 2) % NX

    def at(x_, y_, z_, c_):
        return {"seq": x_ * NZ + z_, "head": y_ * NC + c_}

    def remote(src, dst, send, recv, device):
        return pltpu.make_async_remote_copy(
            src_ref=src, dst_ref=dst, send_sem=send, recv_sem=recv, device_id=device, device_id_type=MESH
        )

    def landed(ref, sem):
        pltpu.make_async_copy(ref, ref, sem).wait()

    barrier = pltpu.get_barrier_semaphore()
    for dz in range(NZ):
        for dy in range(NY):
            if dz or dy:
                pl.semaphore_signal(
                    barrier, inc=1, device_id=at(x, (y + dy) % NY, (z + dz) % NZ, c), device_id_type=MESH
                )
    for device in (at(right, y, z, c), at(left, y, z, c), at(x, y, z, 1 - c)):
        pl.semaphore_signal(barrier, inc=1, device_id=device, device_id_type=MESH)
    pl.semaphore_wait(barrier, NZ * NY - 1 + 3)

    def columns(z_, h):
        return pl.ds(pl.multiple_of((z_ * PER + h) * HEAD, HEAD), HEAD)

    def send(u):
        n, i = UNITS[u]
        z_ = (z + OFFSETS[i]) % NZ
        for h in range(PER):
            src = (k_ref, v_ref, q_ref)[n].at[0, :, columns(z_, h)]
            dst = qs.at[i, y] if n == 2 else kv.at[n, i, x, c, y]
            there = remote(src, dst, send_z.at[n, i], recv_z.at[n, i], at(x, (z_ + 1 + h) % NY, z_, c))
            if i == 0:
                pl.when(mine == h)(lambda: pltpu.make_async_copy(src, dst, recv_z.at[n, i]).start())
                pl.when(mine != h)(lambda: there.start())
            else:
                there.start()

    def sent(u):
        n, i = UNITS[u]
        if i == 0:
            pl.when(active)(lambda: landed(result.at[0, : PER - 1], send_z.at[n, i]))
            pl.when(jnp.logical_not(active))(lambda: landed(result.at[0, :PER], send_z.at[n, i]))
        else:
            landed(result.at[0, :PER], send_z.at[n, i])

    for u in range(WINDOW):
        send(u)

    def along_x(n, i):
        own, half = kv.at[n, i, x, c], NY // 2
        from_left, from_right = kv.at[n, i, left, c, :half], kv.at[n, i, right, c, half:]
        return [
            remote(own, own, send_x.at[n, i], recv_x.at[n, i, 0], at(right, y, z, c)),
            remote(own, own, send_x.at[n, i], recv_x.at[n, i, 0], at(left, y, z, c)),
            remote(from_left, from_left, send_x.at[n, i], recv_x.at[n, i, 1], at(right, y, z, c)),
            remote(from_right, from_right, send_x.at[n, i], recv_x.at[n, i, 1], at(left, y, z, c)),
        ]

    def to_core(n, i, x_):
        ref = kv.at[n, i, x_, c]
        remote(ref, ref, send_c.at[n, i], recv_c.at[n, i], at(x, y, z, 1 - c)).start()

    lane = lax.broadcasted_iota(jnp.int32, (1, HEAD), 1)
    first, last = jnp.zeros((1, HEAD), jnp.int32), jnp.full((1, HEAD), 1 << 20, jnp.int32)
    end = 0
    for n in range(CLIPS):
        start, end = end, end + len_ref[n]
        first = jnp.where(lane == n, start, first)
        last = jnp.where(lane == n, end, last)

    def within(position):
        return (position >= first) & (position < last)

    def far_keys(i):
        row = lax.broadcasted_iota(jnp.int32, (KEYS, HEAD), 0)
        slab = (z + NZ - OFFSETS[i]) % NZ
        position = ((row >> 8) << 11) + (((row >> 5) & 3) << 6) + (((row >> 7) & 1) << 5) + (row & 31) + slab * 256
        far[i] = jnp.where(within(position), 0.0, -FAR).astype(jnp.bfloat16)

    def clip_queries(i):
        row = lax.broadcasted_iota(jnp.int32, (NY * RUN, HEAD), 0)
        slab = (z + NZ - OFFSETS[i]) % NZ
        position = ((row >> 5) << 6) + (row & 31) + (x * 2048 + slab * 256 + c * 32)
        return jnp.where(within(position), 1.0, 0.0).astype(jnp.bfloat16)

    @pl.when(jnp.logical_not(active))
    def _():
        for u in range(len(UNITS)):
            sent(u)
            if u + WINDOW < len(UNITS):
                send(u + WINDOW)

    moved = [u for u in UNITS if u[0] < 2]

    @pl.when(active)
    def _():
        for i in range(NZ):
            far_keys(i)

        def step(t):
            def during(first_step, steps, do):
                if isinstance(t, int):
                    if first_step <= t < first_step + steps:
                        do((t - first_step) // NZ, (t - first_step) % NZ)
                else:
                    pl.when((t >= first_step) & (t < first_step + steps))(
                        lambda: do((t - first_step) // NZ, (t - first_step) % NZ)
                    )

            def begin(n, i):
                landed(kv.at[n, i, x, c], recv_z.at[n, i])
                for copy in along_x(n, i)[:2]:
                    copy.start()
                to_core(n, i, x)

            def forward(n, i):
                landed(kv.at[n, i, :2, c], recv_x.at[n, i, 0])
                for copy in along_x(n, i)[2:]:
                    copy.start()
                to_core(n, i, left)
                to_core(n, i, right)

            def finish(n, i):
                landed(kv.at[n, i, 0, c], recv_x.at[n, i, 1])
                to_core(n, i, across)

            during(0, 2 * NZ, begin)
            during(LAG, 2 * NZ, forward)
            during(2 * LAG, 2 * NZ, finish)

        for t in range(SCORES_AT):
            if t + WINDOW < len(UNITS):
                sent(t)
                send(t + WINDOW)
            step(t)

        for i in range(NZ):
            landed(qs.at[i], recv_z.at[2, i])
        rows = NZ * NY * RUN
        query[:, :HEAD] = qs[...].reshape(rows, HEAD)
        for i in range(NZ):
            query[i * NY * RUN : (i + 1) * NY * RUN, HEAD:] = clip_queries(i)
        top[...] = jnp.full((rows, HEAD), -1e30, jnp.float32)

        @pl.loop(0, NZ)
        def _(i):
            step(SCORES_AT + i)
            landed(kv.at[0, i, :, 1 - c], recv_c.at[0, i])
            key = jnp.concatenate([kv[0, i].reshape(KEYS, HEAD), far[i]], axis=1)
            got = lax.dot_general(query[...], key, (((1,), (1,)), ((), ())), preferred_element_type=jnp.float32)
            score[i] = got
            best = top[...]
            for n in range(KEYS // HEAD):
                best = jnp.maximum(best, got[:, n * HEAD : (n + 1) * HEAD])
            top[...] = best

        for t in range(SCORES_AT + NZ, 2 * NZ + 2 * LAG):
            step(t)
        for i in range(NZ):
            landed(kv.at[1, i, :, 1 - c], recv_c.at[1, i])

    def results(i):
        z_ = (z + NZ - OFFSETS[i]) % NZ
        dst = landing.at[z * PER + mine]
        return [(result.at[i, (y + n) % NY], dst, at(x, (y + n) % NY, z_, c)) for n in range(NY)]

    @pl.when(active)
    def _():
        keys, rows = KEYS_STEP * KEYS, QUERY_STEP * NY * RUN
        for b in reversed(range(NZ // QUERY_STEP)):
            rounds = range(b * QUERY_STEP, (b + 1) * QUERY_STEP)
            block = pl.ds(b * rows, rows)
            highest = jnp.max(top[block], axis=1, keepdims=True)

            def attend(j, total):
                weight = jnp.concatenate(
                    [
                        jnp.exp2((score[j * KEYS_STEP + n, block] - highest) * SCALE).astype(jnp.bfloat16)
                        for n in range(KEYS_STEP)
                    ],
                    axis=1,
                )
                value = kv[1, pl.ds(j * KEYS_STEP, KEYS_STEP)].reshape(keys, HEAD)
                value = jnp.concatenate([value, jnp.ones((keys, HEAD), jnp.bfloat16)], axis=1)
                return total + jnp.dot(weight, value, preferred_element_type=jnp.float32)

            total = lax.fori_loop(0, NZ // KEYS_STEP, attend, jnp.zeros((rows, 2 * HEAD), jnp.float32))
            ready = (total[:, :HEAD] / total[:, HEAD:]).astype(jnp.bfloat16)
            result[b * QUERY_STEP : (b + 1) * QUERY_STEP] = ready.reshape(QUERY_STEP, NY, RUN, HEAD)
            for i in reversed(rounds):
                for n, (src, dst, device) in enumerate(results(i)):
                    there = remote(src, dst, send_o.at[i], recv_o, device)
                    if i == 0 and n == 0:
                        pltpu.make_async_copy(src, dst, recv_o).start()
                    else:
                        there.start()

    landed(landing, recv_o)
    for g in range(NZ * PER):
        out_ref[0, :, g * HEAD : (g + 1) * HEAD] = landing[g]

    @pl.when(active)
    def _():
        for u in range(len(UNITS) - WINDOW, len(UNITS)):
            sent(u)
        for n, i in moved:
            landed(kv.at[n, i, :3, c], send_x.at[n, i])
            landed(kv.at[n, i, :, c], send_c.at[n, i])
        for i in range(NZ):
            landed(result.at[i, : NY - 1] if i == 0 else result.at[i], send_o.at[i])


def shards(queries, keys, values, clip_lengths):
    width = queries.shape[2]
    dma = pltpu.SemaphoreType.DMA
    rows = NZ * NY * RUN
    vmem = pl.BlockSpec(memory_space=pltpu.VMEM)
    return pl.pallas_call(
        kernel,
        out_shape=jax.ShapeDtypeStruct((1, RUN, width), jnp.bfloat16),
        in_specs=[pl.BlockSpec(memory_space=pltpu.SMEM), vmem, vmem, vmem],
        out_specs=vmem,
        scratch_shapes=[
            pltpu.VMEM((2, NZ, NX, NC, NY, RUN, HEAD), jnp.bfloat16),
            pltpu.VMEM((NZ, NY, RUN, HEAD), jnp.bfloat16),
            pltpu.VMEM((NZ, KEYS, HEAD), jnp.bfloat16),
            pltpu.VMEM((rows, 2 * HEAD), jnp.bfloat16),
            pltpu.VMEM((NZ, rows, KEYS), jnp.float32),
            pltpu.VMEM((rows, HEAD), jnp.float32),
            pltpu.VMEM((NZ, NY, RUN, HEAD), jnp.bfloat16),
            pltpu.VMEM((NZ * PER, RUN, HEAD), jnp.bfloat16),
            dma((3, NZ)),
            dma((2, NZ)),
            dma((2, NZ)),
            dma((NZ,)),
            dma((3, NZ)),
            dma((2, NZ, 2)),
            dma((2, NZ)),
            dma,
        ],
        compiler_params=pltpu.CompilerParams(
            collective_id=0, has_side_effects=True, vmem_limit_bytes=56 * 2**20
        ),
        cost_estimate=pl.CostEstimate(flops=2 * 1024 * 8192 * 512, bytes_accessed=2**20, transcendentals=2**23),
    )(clip_lengths, queries, keys, values)


def solution(mesh):
    spec = P(("row", "seq"), "head", None)
    return jax.shard_map(
        shards, mesh=mesh, in_specs=(spec, spec, spec, P("row")), out_specs=spec, check_vma=False
    )
```

```python
import jax
import jax.numpy as jnp
from jax import lax
from jax.experimental import pallas as pl
from jax.experimental.pallas import tpu as pltpu
from jax.sharding import PartitionSpec as P

HEAD = 128
NX, NY, NZ, NC = 4, 4, 8, 2
PER = 3
RUN = 32
CLIPS = 6
OFFSETS = (0, 1, 7, 2, 6, 3, 5, 4)
FAR = 131072.0
SCALE = HEAD**-0.5 * 1.4426950408889634
MESH = pl.DeviceIdType.MESH
KEYS = NX * NC * NY * RUN
KEYS_STEP = 4
QUERY_STEP = 2
UNITS = [(n, i) for n in (0, 2, 1) for i in range(NZ)]
WINDOW = 16
PAIRS = NZ // 2
LAG = 2
SCORES_AT = 6


def kernel(len_ref, q_ref, k_ref, v_ref, out_ref, kv, qs, far, query, score, top, result, landing, *sems):
    send_z, send_x, send_c, send_o, recv_z, recv_x, recv_c, recv_o = sems
    seq, head = lax.axis_index("seq"), lax.axis_index("head")
    x, z = seq // NZ, seq % NZ
    y, c = head // NC, head % NC
    mine = (y + NZ - z - 1) % NY
    active = mine < PER
    right, left, across = (x + 1) % NX, (x + 3) % NX, (x + 2) % NX

    def at(x_, y_, z_, c_):
        return {"seq": x_ * NZ + z_, "head": y_ * NC + c_}

    def remote(src, dst, send, recv, device):
        return pltpu.make_async_remote_copy(
            src_ref=src, dst_ref=dst, send_sem=send, recv_sem=recv, device_id=device, device_id_type=MESH
        )

    def landed(ref, sem):
        pltpu.make_async_copy(ref, ref, sem).wait()

    barrier = pltpu.get_barrier_semaphore()
    for dz in range(NZ):
        for dy in range(NY):
            if dz or dy:
                pl.semaphore_signal(
                    barrier, inc=1, device_id=at(x, (y + dy) % NY, (z + dz) % NZ, c), device_id_type=MESH
                )
    for device in (at(right, y, z, c), at(left, y, z, c), at(x, y, z, 1 - c)):
        pl.semaphore_signal(barrier, inc=1, device_id=device, device_id_type=MESH)
    pl.semaphore_wait(barrier, NZ * NY - 1 + 3)

    def columns(z_, h):
        return pl.ds(pl.multiple_of((z_ * PER + h) * HEAD, HEAD), HEAD)

    def send(u):
        n, i = UNITS[u]
        z_ = (z + OFFSETS[i]) % NZ
        for h in range(PER):
            src = (k_ref, v_ref, q_ref)[n].at[0, :, columns(z_, h)]
            dst = qs.at[i, y] if n == 2 else kv.at[n, i, x, c, y]
            there = remote(src, dst, send_z.at[n, i], recv_z.at[n, i], at(x, (z_ + 1 + h) % NY, z_, c))
            if i == 0:
                pl.when(mine == h)(lambda: pltpu.make_async_copy(src, dst, recv_z.at[n, i]).start())
                pl.when(mine != h)(lambda: there.start())
            else:
                there.start()

    def sent(u):
        n, i = UNITS[u]
        if i == 0:
            pl.when(active)(lambda: landed(result.at[0, : PER - 1], send_z.at[n, i]))
            pl.when(jnp.logical_not(active))(lambda: landed(result.at[0, :PER], send_z.at[n, i]))
        else:
            landed(result.at[0, :PER], send_z.at[n, i])

    for u in range(WINDOW):
        send(u)

    def pair(i):
        return pl.ds(2 * i, 2)

    def along_x(n, i):
        own, half = kv.at[n, pair(i), x, c], NY // 2
        from_left, from_right = kv.at[n, pair(i), left, c, :half], kv.at[n, pair(i), right, c, half:]
        return [
            remote(own, own, send_x.at[n, i], recv_x.at[n, i, 0], at(right, y, z, c)),
            remote(own, own, send_x.at[n, i], recv_x.at[n, i, 0], at(left, y, z, c)),
            remote(from_left, from_left, send_x.at[n, i], recv_x.at[n, i, 1], at(right, y, z, c)),
            remote(from_right, from_right, send_x.at[n, i], recv_x.at[n, i, 1], at(left, y, z, c)),
        ]

    def to_core(n, i, x_):
        ref = kv.at[n, pair(i), x_, c]
        remote(ref, ref, send_c.at[n, i], recv_c.at[n, i], at(x, y, z, 1 - c)).start()

    lane = lax.broadcasted_iota(jnp.int32, (1, HEAD), 1)
    first, last = jnp.zeros((1, HEAD), jnp.int32), jnp.full((1, HEAD), 1 << 20, jnp.int32)
    end = 0
    for n in range(CLIPS):
        start, end = end, end + len_ref[n]
        first = jnp.where(lane == n, start, first)
        last = jnp.where(lane == n, end, last)

    def within(position):
        return (position >= first) & (position < last)

    def far_keys(i):
        row = lax.broadcasted_iota(jnp.int32, (KEYS, HEAD), 0)
        slab = (z + NZ - OFFSETS[i]) % NZ
        position = ((row >> 8) << 11) + (((row >> 5) & 3) << 6) + (((row >> 7) & 1) << 5) + (row & 31) + slab * 256
        far[i] = jnp.where(within(position), 0.0, -FAR).astype(jnp.bfloat16)

    def clip_queries(i):
        row = lax.broadcasted_iota(jnp.int32, (NY * RUN, HEAD), 0)
        slab = (z + NZ - OFFSETS[i]) % NZ
        position = ((row >> 5) << 6) + (row & 31) + (x * 2048 + slab * 256 + c * 32)
        return jnp.where(within(position), 1.0, 0.0).astype(jnp.bfloat16)

    @pl.when(jnp.logical_not(active))
    def _():
        for u in range(len(UNITS)):
            sent(u)
            if u + WINDOW < len(UNITS):
                send(u + WINDOW)

    moved = [(n, i) for n in range(2) for i in range(PAIRS)]

    @pl.when(active)
    def _():
        for i in range(NZ):
            far_keys(i)

        def step(t):
            def during(first_step, steps, do):
                if isinstance(t, int):
                    if first_step <= t < first_step + steps:
                        do((t - first_step) // PAIRS, (t - first_step) % PAIRS)
                else:
                    pl.when((t >= first_step) & (t < first_step + steps))(
                        lambda: do((t - first_step) // PAIRS, (t - first_step) % PAIRS)
                    )

            def begin(n, i):
                landed(kv.at[n, 2 * i, x, c], recv_z.at[n, 2 * i])
                landed(kv.at[n, 2 * i + 1, x, c], recv_z.at[n, 2 * i + 1])
                for copy in along_x(n, i)[:2]:
                    copy.start()
                to_core(n, i, x)

            def forward(n, i):
                landed(kv.at[n, pair(i), :2, c], recv_x.at[n, i, 0])
                for copy in along_x(n, i)[2:]:
                    copy.start()
                to_core(n, i, left)
                to_core(n, i, right)

            def finish(n, i):
                landed(kv.at[n, pair(i), 0, c], recv_x.at[n, i, 1])
                to_core(n, i, across)

            during(0, 2 * PAIRS, begin)
            during(LAG, 2 * PAIRS, forward)
            during(2 * LAG, 2 * PAIRS, finish)

        for t in range(SCORES_AT):
            for u in (2 * t, 2 * t + 1):
                if u + WINDOW < len(UNITS):
                    sent(u)
                    send(u + WINDOW)
            step(t)

        for i in range(NZ):
            landed(qs.at[i], recv_z.at[2, i])
        rows = NZ * NY * RUN
        query[:, :HEAD] = qs[...].reshape(rows, HEAD)
        for i in range(NZ):
            query[i * NY * RUN : (i + 1) * NY * RUN, HEAD:] = clip_queries(i)
        top[...] = jnp.full((rows, HEAD), -1e30, jnp.float32)

        @pl.loop(0, PAIRS)
        def _(j):
            step(SCORES_AT + j)
            landed(kv.at[0, pair(j), :, 1 - c], recv_c.at[0, j])

            @pl.loop(2 * j, 2 * j + 2)
            def _(i):
                key = jnp.concatenate([kv[0, i].reshape(KEYS, HEAD), far[i]], axis=1)
                got = lax.dot_general(query[...], key, (((1,), (1,)), ((), ())), preferred_element_type=jnp.float32)
                score[i] = got
                best = top[...]
                for n in range(KEYS // HEAD):
                    best = jnp.maximum(best, got[:, n * HEAD : (n + 1) * HEAD])
                top[...] = best

        for t in range(SCORES_AT + PAIRS, 2 * PAIRS + 2 * LAG):
            step(t)
        for i in range(PAIRS):
            landed(kv.at[1, pair(i), :, 1 - c], recv_c.at[1, i])

    def results(i):
        z_ = (z + NZ - OFFSETS[i]) % NZ
        dst = landing.at[z * PER + mine]
        return [(result.at[i, (y + n) % NY], dst, at(x, (y + n) % NY, z_, c)) for n in range(NY)]

    @pl.when(active)
    def _():
        keys, rows = KEYS_STEP * KEYS, QUERY_STEP * NY * RUN
        for b in reversed(range(NZ // QUERY_STEP)):
            rounds = range(b * QUERY_STEP, (b + 1) * QUERY_STEP)
            block = pl.ds(b * rows, rows)
            highest = jnp.max(top[block], axis=1, keepdims=True)

            def attend(j, total):
                weight = jnp.concatenate(
                    [
                        jnp.exp2((score[j * KEYS_STEP + n, block] - highest) * SCALE).astype(jnp.bfloat16)
                        for n in range(KEYS_STEP)
                    ],
                    axis=1,
                )
                value = kv[1, pl.ds(j * KEYS_STEP, KEYS_STEP)].reshape(keys, HEAD)
                value = jnp.concatenate([value, jnp.ones((keys, HEAD), jnp.bfloat16)], axis=1)
                return total + jnp.dot(weight, value, preferred_element_type=jnp.float32)

            total = lax.fori_loop(0, NZ // KEYS_STEP, attend, jnp.zeros((rows, 2 * HEAD), jnp.float32))
            ready = (total[:, :HEAD] / total[:, HEAD:]).astype(jnp.bfloat16)
            result[b * QUERY_STEP : (b + 1) * QUERY_STEP] = ready.reshape(QUERY_STEP, NY, RUN, HEAD)
            for i in reversed(rounds):
                for n, (src, dst, device) in enumerate(results(i)):
                    there = remote(src, dst, send_o.at[i], recv_o, device)
                    if i == 0 and n == 0:
                        pltpu.make_async_copy(src, dst, recv_o).start()
                    else:
                        there.start()

    landed(landing, recv_o)
    for g in range(NZ * PER):
        out_ref[0, :, g * HEAD : (g + 1) * HEAD] = landing[g]

    @pl.when(active)
    def _():
        for u in range(len(UNITS) - WINDOW, len(UNITS)):
            sent(u)
        for n, i in moved:
            landed(kv.at[n, pair(i), :3, c], send_x.at[n, i])
            landed(kv.at[n, pair(i), :, c], send_c.at[n, i])
        for i in range(NZ):
            landed(result.at[i, : NY - 1] if i == 0 else result.at[i], send_o.at[i])


def shards(queries, keys, values, clip_lengths):
    width = queries.shape[2]
    dma = pltpu.SemaphoreType.DMA
    rows = NZ * NY * RUN
    vmem = pl.BlockSpec(memory_space=pltpu.VMEM)
    return pl.pallas_call(
        kernel,
        out_shape=jax.ShapeDtypeStruct((1, RUN, width), jnp.bfloat16),
        in_specs=[pl.BlockSpec(memory_space=pltpu.SMEM), vmem, vmem, vmem],
        out_specs=vmem,
        scratch_shapes=[
            pltpu.VMEM((2, NZ, NX, NC, NY, RUN, HEAD), jnp.bfloat16),
            pltpu.VMEM((NZ, NY, RUN, HEAD), jnp.bfloat16),
            pltpu.VMEM((NZ, KEYS, HEAD), jnp.bfloat16),
            pltpu.VMEM((rows, 2 * HEAD), jnp.bfloat16),
            pltpu.VMEM((NZ, rows, KEYS), jnp.float32),
            pltpu.VMEM((rows, HEAD), jnp.float32),
            pltpu.VMEM((NZ, NY, RUN, HEAD), jnp.bfloat16),
            pltpu.VMEM((NZ * PER, RUN, HEAD), jnp.bfloat16),
            dma((3, NZ)),
            dma((2, PAIRS)),
            dma((2, PAIRS)),
            dma((NZ,)),
            dma((3, NZ)),
            dma((2, PAIRS, 2)),
            dma((2, PAIRS)),
            dma,
        ],
        compiler_params=pltpu.CompilerParams(
            collective_id=0, has_side_effects=True, vmem_limit_bytes=56 * 2**20
        ),
        cost_estimate=pl.CostEstimate(flops=2 * 1024 * 8192 * 512, bytes_accessed=2**20, transcendentals=2**23),
    )(clip_lengths, queries, keys, values)


def solution(mesh):
    spec = P(("row", "seq"), "head", None)
    return jax.shard_map(
        shards, mesh=mesh, in_specs=(spec, spec, spec, P("row")), out_specs=spec, check_vma=False
    )
```
